32 devices in a mesh: tm: 8 (over y, x, core), sub: 4 (over z).
Axes of the slice: x: 2, y: 2, z: 4, core: 2. Of those that a mesh axis runs over, the one named last changes fastest.
Arguments:
- feature_maps: bfloat16 [128, 30, 40, 128], P(('tm', 'sub')), may hold values from -6 to 6
- context_maps: bfloat16 [128, 2, 40, 128], P(('tm', 'sub')), may hold values from -6 to 6
- hidden_state: bfloat16 [544, 2, 40, 128], P(('tm', 'sub')), may hold values from -1 to 1
- lookup_grid: int32 [544, 2, 40], P(('tm', 'sub')), may hold values from 41 to 1158, as said below
- loop_edges: int32 [32, 2], P(('tm', 'sub')), may hold values from 0 to 127, as said below
- inverse_depth: float32 [128, 2, 40], P(('tm', 'sub')), may hold values from 0.2 to 2
- translations: float32 [3, 128], replicated, may hold values from -2 to 2
- update_reset_weight: bfloat16 [3, 3, 256, 256], replicated, may hold values from -0.125 to 0.125
- update_reset_bias: float32 [256], replicated, may hold values from -4 to 4
- candidate_weight: bfloat16 [3, 3, 256, 128], replicated, may hold values from -0.125 to 0.125
- candidate_bias: float32 [128], replicated, may hold values from -3 to 3
- correlation_weight: float32 [9, 128], replicated, may hold values from -2 to 2
- flow_weight: float32 [2, 128], replicated, may hold values from -4 to 4
- motion_bias: float32 [128], replicated, may hold values from -3 to 3
- head_weight: bfloat16 [128, 4], replicated, may hold values from -0.5 to 0.5
- head_bias: float32 [4], replicated, may hold values from -3 to 3
Outputs:
- correlation: float32 [544, 9, 2, 40], P(('tm', 'sub'))
- new_hidden: bfloat16 [544, 2, 40, 128], P(('tm', 'sub'))
- revision: float32 [544, 4, 2, 40], P(('tm', 'sub'))
- pose_block: float32 [544, 6, 6], P(('tm', 'sub'))
- pose_gradient: float32 [544, 6], P(('tm', 'sub'))
- depth_pose: float32 [544, 6, 2, 40], P(('tm', 'sub'))
- depth_diagonal: float32 [128, 2, 2, 40], P(('tm', 'sub'))
The draws below stay inside these ranges and needn't reach their ends.
Inputs may be any that keep to these rules, and one draw needn't show every extreme that they name: `lookup_grid`: each value is a pixel r * 40 + c with 1 <= r <= 28 and 1 <= c <= 38. loop_edges[b, 0] is a keyframe of block b; the targets loop_edges[b, 1] lie anywhere, at most 4 of them in any one block, and some block receives exactly 4.
All inputs are finite; a program needn't handle non-finite values.
Results may differ from the reference program's by a relative error of at most 0.0042.
Values may be sent and summed in bfloat16 or wider, within the bound.
A program may use at most 64 MiB of HBM per device.

```python
import math
import jax
import jax.numpy as jnp
import numpy as np
from jax import lax

CHANNELS = 128
HIDDEN_SIZE = 128
HEIGHT = 30
WIDTH = 40
KEYFRAMES = 4
QUERY_ROWS = 2
LOOP_MOST = 4
LOOPS = 32
FRAMES = 128
EDGES = 544


def draw_lookup_grid(key, part):
    key_rows = jax.random.fold_in(key, 11)
    key_cols = jax.random.fold_in(key, 12)
    shape = (EDGES, QUERY_ROWS, WIDTH)
    grid_rows = jax.random.randint(key_rows, shape, 1, HEIGHT - 1)
    grid_cols = jax.random.randint(key_cols, shape, 1, WIDTH - 1)
    flat_grid = grid_rows * WIDTH + grid_cols
    flat_grid = flat_grid.at[0, 0, 0].set(WIDTH + 1)
    flat_grid = flat_grid.at[EDGES - 1, QUERY_ROWS - 1, WIDTH - 1].set(HEIGHT * WIDTH - WIDTH - 2)
    return flat_grid.astype(jnp.int32)


def draw_loop_edges(key, part):
    block_order = jax.random.permutation(jax.random.fold_in(key, 21), LOOPS)
    slot_ids = jnp.arange(LOOPS, dtype=jnp.int32)
    chosen_rank = jnp.where(slot_ids < LOOP_MOST, 0, slot_ids - LOOP_MOST + 1)
    multiset = block_order[chosen_rank]
    assignment = jax.random.permutation(jax.random.fold_in(key, 22), LOOPS)
    target_block = multiset[assignment]
    busiest = block_order[0]
    holder = jnp.argmax((assignment == 0).astype(jnp.int32)).astype(jnp.int32)
    opposite = ((busiest + LOOPS // 2) % LOOPS).astype(jnp.int32)
    displaced = target_block[opposite]
    target_block = target_block.at[holder].set(displaced)
    target_block = target_block.at[opposite].set(busiest)
    source_frame = slot_ids * KEYFRAMES + jax.random.randint(jax.random.fold_in(key, 23), (LOOPS,), 0, KEYFRAMES)
    target_frame = target_block * KEYFRAMES + jax.random.randint(jax.random.fold_in(key, 24), (LOOPS,), 0, KEYFRAMES)
    return jnp.stack([source_frame, target_frame], axis=1).astype(jnp.int32)


def shard_levels(own_key, shape, pieces, smallest, top_value):
    factor_of = 1.0
    for dim, parts in pieces:
        steps = jax.random.uniform(jax.random.fold_in(jax.random.fold_in(own_key, 6), dim), (parts,), jnp.float32, smallest / len(pieces), top_value / len(pieces))
        factor_of = factor_of * jnp.repeat(jnp.exp(steps), shape[dim] // parts).reshape((-1,) + (1,) * (len(shape) - 1 - dim))
    return factor_of


def noise(key, dims, spread, reach, split=(), kind=jnp.bfloat16):
    values = spread * jax.random.normal(key, dims, jnp.float32)
    if split:
        values = values * shard_levels(key, dims, split, -0.22, 0.18)
    return jnp.clip(values, -reach, reach).astype(kind)


def setup_inputs(seed: int = 0) -> dict:
    key_of = jax.random.split(jax.random.key(seed), 17)
    feature_maps = noise(key_of[0], (FRAMES, HEIGHT, WIDTH, CHANNELS), 1.0, 6.0, ((0, 32),))
    context_maps = noise(key_of[1], (FRAMES, QUERY_ROWS, WIDTH, HIDDEN_SIZE), 1.0, 6.0, ((0, 32),))
    hidden_state = jnp.clip(jax.random.uniform(key_of[2], (EDGES, QUERY_ROWS, WIDTH, HIDDEN_SIZE), jnp.float32, -1.0, 1.0) * shard_levels(key_of[2], (EDGES, QUERY_ROWS, WIDTH, HIDDEN_SIZE), ((0, 32),), -0.4, 0.0), -1.0, 1.0).astype(jnp.bfloat16)
    lookup_grid = draw_lookup_grid(jax.random.fold_in(key_of[16], 71), 0)
    loop_edges = draw_loop_edges(jax.random.fold_in(key_of[16], 71), 0)
    inverse_depth = jnp.clip(jnp.exp(math.log(2.0) - 2.3025851 * jax.random.uniform(key_of[5], (FRAMES, QUERY_ROWS, WIDTH), jnp.float32) ** shard_levels(key_of[5], (FRAMES, QUERY_ROWS, WIDTH), ((0, 32),), -0.2, 0.2)), 0.2, 2.0)
    translations = noise(key_of[6], (3, FRAMES), 0.3, 2.0, (), jnp.float32)
    update_reset_weight = noise(key_of[7], (3, 3, 2 * HIDDEN_SIZE, 2 * HIDDEN_SIZE), (18 * HIDDEN_SIZE) ** -0.5, 0.125)
    update_reset_bias = noise(key_of[8], (2 * HIDDEN_SIZE,), 1.0, 4.0, (), jnp.float32)
    candidate_weight = noise(key_of[9], (3, 3, 2 * HIDDEN_SIZE, HIDDEN_SIZE), (18 * HIDDEN_SIZE) ** -0.5, 0.125)
    candidate_bias = noise(key_of[10], (HIDDEN_SIZE,), 0.5, 3.0, (), jnp.float32)
    correlation_weight = noise(key_of[11], (9, HIDDEN_SIZE), 9 ** -0.5, 2.0, (), jnp.float32)
    flow_weight = noise(key_of[12], (2, HIDDEN_SIZE), 2 ** -0.5, 4.0, (), jnp.float32)
    motion_bias = noise(key_of[13], (HIDDEN_SIZE,), 0.5, 3.0, (), jnp.float32)
    head_weight = noise(key_of[14], (HIDDEN_SIZE, 4), HIDDEN_SIZE ** -0.5, 0.5)
    head_bias = noise(key_of[15], (4,), 1.0, 3.0, (), jnp.float32)
    return {"feature_maps": feature_maps, "context_maps": context_maps, "hidden_state": hidden_state, "lookup_grid": lookup_grid, "loop_edges": loop_edges, "inverse_depth": inverse_depth, "translations": translations, "update_reset_weight": update_reset_weight, "update_reset_bias": update_reset_bias, "candidate_weight": candidate_weight, "candidate_bias": candidate_bias, "correlation_weight": correlation_weight, "flow_weight": flow_weight, "motion_bias": motion_bias, "head_weight": head_weight, "head_bias": head_bias}


focal = 40.0
highest = lax.Precision.HIGHEST
neighbour_steps = (-2, -1, 1, 2)

def window_steps(stride):
    return np.array([row_step * stride + col_step for row_step in (-1, 0, 1) for col_step in (-1, 0, 1)], dtype=np.int32)

def conv_same(inputs, weight):
    padded = jnp.pad(inputs, ((0, 0), (1, 1), (1, 1), (0, 0))).astype(jnp.float32)
    batch_size, out_rows, out_cols = (inputs.shape[0], inputs.shape[1], inputs.shape[2])
    weight_float = weight.astype(jnp.float32)
    accumulated = jnp.zeros((batch_size * out_rows * out_cols, weight.shape[-1]), jnp.float32)
    for row_step in range(3):
        for col_step in range(3):
            window = padded[:, row_step:row_step + out_rows, col_step:col_step + out_cols, :]
            accumulated = accumulated + jnp.dot(window.reshape(-1, window.shape[-1]), weight_float[row_step, col_step], precision=highest)
    return accumulated.reshape(batch_size, out_rows, out_cols, weight.shape[-1])

def reference(feature_maps, context_maps, hidden_state, lookup_grid, loop_edges, inverse_depth, translations, update_reset_weight, update_reset_bias, candidate_weight, candidate_bias, correlation_weight, flow_weight, motion_bias, head_weight, head_bias):
    frame_count = feature_maps.shape[0]
    block_count = frame_count // KEYFRAMES
    edges_block = 4 * KEYFRAMES + 1
    pixels = QUERY_ROWS * WIDTH
    scale = 1.0 / math.sqrt(CHANNELS)
    steps = jnp.asarray(window_steps(WIDTH))
    near_frame = np.repeat(np.arange(KEYFRAMES), 4).astype(np.int32)
    near_step = np.tile(np.array(neighbour_steps, dtype=np.int32), KEYFRAMES).astype(np.int32)
    frames_flat = feature_maps.reshape(frame_count * HEIGHT * WIDTH, CHANNELS)
    pixel_index = jnp.arange(pixels, dtype=jnp.int32)
    pixel_col = pixel_index % WIDTH
    pixel_row = pixel_index // WIDTH
    column_coord = (pixel_col.astype(jnp.float32) - (WIDTH - 1) / 2.0) / focal
    row_coord = (pixel_row.astype(jnp.float32) - (HEIGHT - 1) / 2.0) / focal

    def one_block(block_id):
        first_frame = (block_id * KEYFRAMES).astype(jnp.int32)
        loop_pair = lax.dynamic_slice_in_dim(loop_edges, block_id, 1, 0)[0]
        source = jnp.concatenate([first_frame + jnp.asarray(near_frame), loop_pair[0:1]])
        target = jnp.concatenate([first_frame + jnp.asarray(near_frame + near_step), loop_pair[1:2]])
        valid = ((target >= 0) & (target < frame_count)).astype(jnp.float32)
        safe_target = jnp.clip(target, 0, frame_count - 1)
        grid = lax.dynamic_slice_in_dim(lookup_grid, block_id * edges_block, edges_block, 0).reshape(edges_block, pixels)
        queries = feature_maps[source, :QUERY_ROWS].reshape(edges_block, pixels, CHANNELS)
        index = safe_target[:, None, None] * (HEIGHT * WIDTH) + grid[:, None, :] + steps[None, :, None]
        gathered = frames_flat[index]
        correlation = jnp.einsum('ejpc,epc->ejp', gathered.astype(jnp.float32), queries.astype(jnp.float32), precision=highest) * scale * valid[:, None, None]
        grid_col = grid % WIDTH
        grid_row = grid // WIDTH
        flow_u = (grid_col - pixel_col[None, :]).astype(jnp.float32) / focal
        flow_v = (grid_row - pixel_row[None, :]).astype(jnp.float32) / focal
        motion = jax.nn.relu(jnp.einsum('ejp,jh->eph', correlation, correlation_weight, precision=highest) + flow_u[..., None] * flow_weight[0] + flow_v[..., None] * flow_weight[1] + motion_bias)
        context = context_maps[source].reshape(edges_block, pixels, HIDDEN_SIZE)
        inputs = (motion + context.astype(jnp.float32)).astype(jnp.bfloat16).reshape(edges_block, QUERY_ROWS, WIDTH, HIDDEN_SIZE)
        hidden = lax.dynamic_slice_in_dim(hidden_state, block_id * edges_block, edges_block, 0)
        gates = jax.nn.sigmoid(conv_same(jnp.concatenate([hidden, inputs], axis=-1), update_reset_weight) + update_reset_bias)
        update = gates[..., :HIDDEN_SIZE]
        reset = gates[..., HIDDEN_SIZE:]
        gated = (reset * hidden.astype(jnp.float32)).astype(jnp.bfloat16)
        candidate = jnp.tanh(conv_same(jnp.concatenate([gated, inputs], axis=-1), candidate_weight) + candidate_bias)
        new_hidden = ((1.0 - update) * hidden.astype(jnp.float32) + update * candidate).astype(jnp.bfloat16)
        head = jnp.dot(new_hidden.reshape(-1, HIDDEN_SIZE).astype(jnp.float32), head_weight.astype(jnp.float32), precision=highest) + head_bias
        head = head.reshape(edges_block, pixels, 4)
        delta_u = head[..., 0]
        delta_v = head[..., 1]
        weight_u = jax.nn.sigmoid(head[..., 2])
        weight_v = jax.nn.sigmoid(head[..., 3])
        revision = jnp.stack([delta_u, delta_v, weight_u, weight_v], axis=1)
        depth = inverse_depth[source].reshape(edges_block, pixels)
        shift = translations[:, safe_target] - translations[:, source]
        shift_x = shift[0][:, None]
        shift_y = shift[1][:, None]
        shift_z = shift[2][:, None]
        col_c = jnp.broadcast_to(column_coord[None, :], (edges_block, pixels))
        row_c = jnp.broadcast_to(row_coord[None, :], (edges_block, pixels))
        target_u = (grid_col.astype(jnp.float32) - (WIDTH - 1) / 2.0) / focal + delta_u
        target_v = (grid_row.astype(jnp.float32) - (HEIGHT - 1) / 2.0) / focal + delta_v
        resid_u = target_u - (col_c + depth * (shift_x - col_c * shift_z))
        resid_v = target_v - (row_c + depth * (shift_y - row_c * shift_z))
        zeros_here = jnp.zeros_like(depth)
        jac_u = jnp.stack([depth, zeros_here, -col_c * depth, -col_c * row_c, 1.0 + col_c * col_c, -row_c])
        jac_v = jnp.stack([zeros_here, depth, -row_c * depth, -(1.0 + row_c * row_c), col_c * row_c, col_c])
        depth_u = shift_x - col_c * shift_z
        depth_v = shift_y - row_c * shift_z
        scaled_u = weight_u * valid[:, None]
        scaled_v = weight_v * valid[:, None]
        pose_block = jnp.einsum('aep,bep->eab', jac_u * scaled_u, jac_u, precision=highest) + jnp.einsum('aep,bep->eab', jac_v * scaled_v, jac_v, precision=highest)
        pose_gradient = jnp.einsum('aep,ep->ea', jac_u * scaled_u, resid_u, precision=highest) + jnp.einsum('aep,ep->ea', jac_v * scaled_v, resid_v, precision=highest)
        depth_pose = (jac_u * (scaled_u * depth_u) + jac_v * (scaled_v * depth_v)).transpose(1, 0, 2)
        curvature = scaled_u * depth_u * depth_u + scaled_v * depth_v * depth_v
        slope = scaled_u * depth_u * resid_u + scaled_v * depth_v * resid_v
        owner = ((source - first_frame)[:, None] == jnp.arange(KEYFRAMES, dtype=jnp.int32)[None, :]).astype(jnp.float32)
        depth_diagonal = jnp.stack([jnp.einsum('ek,ep->kp', owner, curvature, precision=highest), jnp.einsum('ek,ep->kp', owner, slope, precision=highest)], axis=1)
        return (correlation, new_hidden, revision, pose_block, pose_gradient, depth_pose, depth_diagonal)
    results = lax.map(one_block, jnp.arange(block_count, dtype=jnp.int32))
    edge_total = block_count * edges_block
    return (results[0].reshape(edge_total, 9, QUERY_ROWS, WIDTH), results[1].reshape(edge_total, QUERY_ROWS, WIDTH, HIDDEN_SIZE), results[2].reshape(edge_total, 4, QUERY_ROWS, WIDTH), results[3].reshape(edge_total, 6, 6), results[4].reshape(edge_total, 6), results[5].reshape(edge_total, 6, QUERY_ROWS, WIDTH), results[6].reshape(frame_count, 2, QUERY_ROWS, WIDTH))
```

```python
import functools
import math

import jax
import jax.numpy as jnp
from jax import lax
from jax.experimental import pallas as pl
from jax.experimental.pallas import tpu as pltpu
from jax.sharding import PartitionSpec as P

HEIGHT = 30
WIDTH = 40
KEYFRAMES = 4
QUERY_ROWS = 2
LOOP_MOST = 4
PIXELS = QUERY_ROWS * WIDTH
FRAME_PIXELS = HEIGHT * WIDTH
NEAR = 4 * KEYFRAMES
EDGES = NEAR + 1
LANES = 128
TAPS = 9
MESH = pl.DeviceIdType.MESH
VMEM = pltpu.VMEM
bf16 = jnp.bfloat16
f32 = jnp.float32
highest = lax.Precision.HIGHEST
neighbour_steps = (-2, -1, 1, 2)

TO_PREV = ((0, 0, 2), (1, 0, 3), (4, 1, 3))
TO_NEXT = ((11, 2, 0), (14, 3, 0), (15, 3, 1))
QUERY_MSG = 2 * PIXELS + 16
LOOP_MSG = PIXELS + 16


def params(collective_id=None):
    return pltpu.CompilerParams(
        collective_id=collective_id,
        has_side_effects=collective_id is not None,
        vmem_limit_bytes=48 * 1024 * 1024,
    )


def places(tm_count, sub_count):
    tm, sub = lax.axis_index("tm"), lax.axis_index("sub")
    block = tm * sub_count + sub
    total = tm_count * sub_count
    after = lax.rem(block + 1, total)
    before = lax.rem(block + total - 1, total)
    coords = lambda b: (b // sub_count, lax.rem(b, sub_count))
    line = [(lax.rem(tm + d, tm_count), sub) for d in range(1, tm_count)]
    column = [(tm, lax.rem(sub + d, sub_count)) for d in range(1, sub_count)]
    return tm, sub, coords(before), coords(after), line, column


def greet(peers):
    barrier = pltpu.get_barrier_semaphore()
    for peer in peers:
        pl.semaphore_signal(barrier, inc=1, device_id=peer, device_id_type=MESH)
    pl.semaphore_wait(barrier, len(peers))


def send(src, dst, send_sem, recv_sem, peer):
    copy = pltpu.make_async_remote_copy(
        src_ref=src, dst_ref=dst, send_sem=send_sem, recv_sem=recv_sem,
        device_id=peer, device_id_type=MESH,
    )
    copy.start()
    return copy


def queries_out(tm_count, sub_count, to_prev, to_next, loop, from_prev, from_next, chosen,
                got_prev, got_next, line, slots, cands, near_sem, line_sem, sub_sem):
    tm, sub, before, after, line_peers, column = places(tm_count, sub_count)
    greet([before, after] + line_peers + column)
    line_copies = [
        send(loop, line.at[d + 1], line_sem.at[0, d], line_sem.at[1, d], peer)
        for d, peer in enumerate(line_peers)
    ]
    near_copies = [
        send(to_next, got_prev, near_sem.at[0, 0], near_sem.at[1, 0], after),
        send(to_prev, got_next, near_sem.at[0, 1], near_sem.at[1, 1], before),
    ]
    line[0] = loop[...]
    slots[...] = jnp.zeros_like(slots)
    here = tm.astype(f32)
    subs = [lax.rem(sub + e, sub_count).astype(f32) for e in range(sub_count)]
    for copy in line_copies:
        copy.wait()

    def pick(d, counts):
        message = line[d]
        facts = message[PIXELS:].astype(f32)
        mine = facts[2:3] == here
        new = []
        for e in range(sub_count):
            match = (mine & (facts[3:4] == subs[e])).astype(f32)
            for k in range(LOOP_MOST):
                take = jnp.where(counts[e] == float(k), match, 0.0)
                slots[e, k] += (message.astype(f32) * take).astype(bf16)
            new.append(counts[e] + match)
        return tuple(new)

    zero = jnp.zeros((1, LANES), f32)
    lax.fori_loop(0, tm_count, pick, (zero,) * sub_count)
    sub_copies = [
        send(slots.at[e + 1], cands.at[e + 1], sub_sem.at[0, e], sub_sem.at[1, e], peer)
        for e, peer in enumerate(column)
    ]
    cands[0] = slots[0]
    chosen[...] = jnp.zeros_like(chosen)
    for copy in sub_copies:
        copy.wait()

    def compact(e, count):
        for k in range(LOOP_MOST):
            message = cands[e, k].astype(f32)
            there = message[PIXELS + 7 : PIXELS + 8]
            for m in range(LOOP_MOST):
                take = jnp.where(count == float(m), there, 0.0)
                chosen[m] += (message * take).astype(bf16)
            count = count + there
        return count

    lax.fori_loop(0, sub_count, compact, zero)
    for copy in near_copies:
        copy.wait()
    from_prev[...] = got_prev[...]
    from_next[...] = got_next[...]


def results_back(tm_count, sub_count, to_prev, to_next, loops, near_prev, near_next, loop_corr,
                 got_prev, got_next, pool, backs, lines, near_sem, line_sem, sub_sem):
    tm, sub, before, after, line_peers, column = places(tm_count, sub_count)
    greet([before, after] + line_peers + column)
    sub_copies = [
        send(loops, pool.at[e + 1], sub_sem.at[0, e], sub_sem.at[1, e], peer)
        for e, peer in enumerate(column)
    ]
    near_copies = [
        send(to_next, got_prev, near_sem.at[0, 0], near_sem.at[1, 0], after),
        send(to_prev, got_next, near_sem.at[0, 1], near_sem.at[1, 1], before),
    ]
    pool[0] = loops[...]
    backs[...] = jnp.zeros_like(backs)
    own = sub.astype(f32)
    for copy in sub_copies:
        copy.wait()

    def pick(d, carry):
        wanted = lax.rem(tm + d, tm_count).astype(f32)
        for e in range(sub_count):
            for k in range(LOOP_MOST):
                found = pool[e, k]
                match = (found[9:10] == wanted) & (found[10:11] == own)
                backs[d] += found * jnp.where(match, found[11:12], 0.0)
        return carry

    lax.fori_loop(0, tm_count, pick, 0)
    line_copies = [
        send(backs.at[d + 1], lines.at[d + 1], line_sem.at[0, d], line_sem.at[1, d], peer)
        for d, peer in enumerate(line_peers)
    ]
    lines[0] = backs[0]
    for copy in line_copies:
        copy.wait()
    total = lines[0]
    for d in range(1, tm_count):
        total = total + lines[d]
    loop_corr[...] = total
    for copy in near_copies:
        copy.wait()
    near_prev[...] = got_prev[...]
    near_next[...] = got_next[...]


def tap_steps(shape):
    k = lax.broadcasted_iota(jnp.int32, shape, 1)
    row = jnp.where(k >= 6, 1, jnp.where(k >= 3, 0, -1))
    step = row * WIDTH + (k - 3 * (row + 1) - 1)
    return jnp.where(k < TAPS, step, 0)


def correlate(features, queries, grid, from_prev, from_next, chosen, near, to_prev, to_next, loops):
    scale = 1.0 / math.sqrt(features.shape[-1])
    rows = lax.broadcasted_iota(jnp.int32, (16, LANES), 0)

    def split_grid(facts):
        return facts[0:1].astype(f32) * float(WIDTH) + facts[1:2].astype(f32)

    grids = [grid[e : e + 1].astype(f32) for e in range(NEAR)]
    pairs = [[] for _ in range(KEYFRAMES)]
    for i in range(KEYFRAMES):
        for n, step in enumerate(neighbour_steps):
            if 0 <= i + step < KEYFRAMES:
                pairs[i + step].append((queries[i], grids[4 * i + n], near, 4 * i + n))
    for refs, edges, low, out in ((from_prev, TO_NEXT, 2, to_next), (from_next, TO_PREV, 0, to_prev)):
        for n, (_, source, target) in enumerate(edges):
            q = refs[(source - low) * PIXELS : (source - low + 1) * PIXELS]
            facts = refs[2 * PIXELS : 2 * PIXELS + 16].astype(f32)
            pairs[target].append((q, split_grid(facts[2 * n : 2 * n + 2]), out, n))

    def look_up(q, pixel_rows, frame):
        count = len(pixel_rows)
        stacked = jnp.concatenate(pixel_rows + [jnp.zeros((8 - count % 8, LANES), f32)], axis=0)
        columns = jnp.transpose(stacked)
        index = jnp.concatenate(
            [
                jnp.broadcast_to(columns[:PIXELS, n : n + 1], (PIXELS, LANES)).astype(jnp.int32)
                for n in range(count)
            ],
            axis=0,
        )
        index = index + tap_steps(index.shape)
        found = jnp.zeros(index.shape, f32)
        for start in range(0, FRAME_PIXELS, LANES):
            base = min(start, FRAME_PIXELS - LANES)
            part = frame[pl.ds(base, LANES), :]
            volume = lax.dot_general(q, part, (((1,), (1,)), ((), ())), preferred_element_type=f32)
            local = index - base
            inside = (index >= start) & (index < start + LANES)
            picked = jnp.take_along_axis(volume, local & (LANES - 1), axis=1)
            found = jnp.where(inside, picked, found)
        found = found * scale
        return [jnp.transpose(found[n * PIXELS : (n + 1) * PIXELS])[:16] for n in range(count)]

    pad = lambda row: jnp.concatenate([row, jnp.zeros((1, LANES - PIXELS), f32)], axis=1)
    for j in range(KEYFRAMES):
        q = jnp.concatenate([p[0] for p in pairs[j]], axis=0)
        pixel_rows = [p[1] if p[1].shape[1] == LANES else pad(p[1]) for p in pairs[j]]
        for result, (_, _, out, n) in zip(look_up(q, pixel_rows, features.at[j]), pairs[j]):
            out[n, :, :PIXELS] = result
            out[n, :, PIXELS:] = jnp.zeros((16, LANES - PIXELS), f32)

    for k in range(LOOP_MOST):
        facts = chosen[k, PIXELS:].astype(f32)
        frame = jnp.max(facts[4:5]).astype(jnp.int32)
        (result,) = look_up(chosen[k, :PIXELS], [split_grid(facts[0:2])], features.at[frame])
        result = jnp.concatenate([result, jnp.zeros((16, LANES - PIXELS), f32)], axis=1)
        for row, fact in ((9, 5), (10, 6), (11, 7)):
            result = jnp.where(rows == row, jnp.broadcast_to(facts[fact : fact + 1], (16, LANES)), result)
        loops[k] = result


def sigmoid(x):
    return 0.5 * jnp.tanh(0.5 * x) + 0.5


def update(frame_total, near, near_prev, near_next, loop_corr, hidden, context, grid, depth, moves, ends, first_ref,
           gate_weight, gate_bias, cand_weight, cand_bias, enc_weight, head_weight, head_bias,
           correlation, new_hidden, revision, pose, depth_pose, depth_diagonal,
           taps, inputs, heads, sources, shifts):
    first = first_ref[0]
    loop_source = ends[0, 0] - first
    targets, valids = [], []
    for e in range(EDGES):
        if e < NEAR:
            source = first + e // 4
            target = first + e // 4 + neighbour_steps[e % 4]
        else:
            source, target = ends[0, 0], ends[0, 1]
        ok = jnp.where((target >= 0) & (target < frame_total), 1.0, 0.0).astype(f32)
        safe = jnp.clip(target, 0, frame_total - 1)
        for a in range(3):
            shifts[a, e : e + 1, :] = jnp.full((1, LANES), moves[a, safe] - moves[a, source], f32)
        shifts[3, e : e + 1, :] = jnp.full((1, LANES), ok, f32)
        valids.append(ok)
    shift_x, shift_y, shift_z, valid = [shifts[a, :EDGES, :PIXELS] for a in range(4)]

    lane = lax.broadcasted_iota(jnp.int32, (EDGES, PIXELS), 1)
    pixel_row = jnp.where(lane >= WIDTH, 1, 0)
    pixel_col = (lane - WIDTH * pixel_row).astype(f32)
    pixel_row = pixel_row.astype(f32)
    flat = grid[...].astype(f32)
    grid_row = jnp.floor((flat + 0.5) * (1.0 / WIDTH))
    grid_col = flat - float(WIDTH) * grid_row
    flow_u = (grid_col - pixel_col) / 40.0
    flow_v = (grid_row - pixel_row) / 40.0

    crossing = {e: near_next[n] for n, (e, _, _) in enumerate(TO_NEXT)}
    crossing.update({e: near_prev[n] for n, (e, _, _) in enumerate(TO_PREV)})
    low = lax.broadcasted_iota(jnp.int32, (16, PIXELS), 0)
    for e in range(EDGES):
        found = loop_corr[...] if e == NEAR else crossing[e] if e in crossing else near[e]
        found = found[:, :PIXELS] * valids[e]
        correlation[e] = found[:TAPS]
        rows = jnp.where(low < TAPS, found, 0.0)
        rows = jnp.where(low == 9, jnp.broadcast_to(flow_u[e : e + 1], rows.shape), rows)
        rows = jnp.where(low == 10, jnp.broadcast_to(flow_v[e : e + 1], rows.shape), rows)
        rows = jnp.where(low == 11, 1.0, rows)
        motion = lax.dot_general(
            rows, enc_weight[...], (((0,), (0,)), ((), ())), precision=highest, preferred_element_type=f32
        )
        about = context[e // 4 if e < NEAR else loop_source].astype(f32)
        inputs[e] = (jax.nn.relu(motion) + about).astype(bf16).astype(f32)
        sources[e : e + 1, :PIXELS] = depth[pl.ds(e // 4 if e < NEAR else loop_source, 1), :]

    def halves(x):
        return x[:, :WIDTH].reshape(-1, LANES), x[:, WIDTH:].reshape(-1, LANES)

    count = EDGES * WIDTH
    col = lax.broadcasted_iota(jnp.int32, (EDGES, WIDTH, LANES), 1).reshape(count, LANES)

    def around(x):
        left = jnp.where(col == 0, 0.0, pltpu.roll(x, 1, 0))
        right = jnp.where(col == WIDTH - 1, 0.0, pltpu.roll(x, count - 1, 0))
        return left.astype(bf16), x.astype(bf16), right.astype(bf16)

    hid = halves(hidden[...].astype(f32))
    inp = halves(inputs[...])
    for r in range(2):
        for b, value in enumerate(around(hid[r])):
            taps[r, :, 2 * b * LANES : (2 * b + 1) * LANES] = value
        for b, value in enumerate(around(inp[r])):
            taps[r, :, (2 * b + 1) * LANES : (2 * b + 2) * LANES] = value
    dot = functools.partial(jnp.dot, preferred_element_type=f32)
    keep = []
    gated = []
    for r in range(2):
        gates = dot(taps[0], gate_weight[1 - r]) + dot(taps[1], gate_weight[2 - r]) + gate_bias[...]
        gates = sigmoid(gates)
        keep.append(gates[:, :LANES])
        gated.append((gates[:, LANES:] * hid[r]).astype(bf16).astype(f32))
    for r in range(2):
        for b, value in enumerate(around(gated[r])):
            taps[r, :, 2 * b * LANES : (2 * b + 1) * LANES] = value
    both = dot(taps[0], jnp.concatenate([cand_weight[1], cand_weight[0]], axis=1))
    both = both + dot(taps[1], jnp.concatenate([cand_weight[2], cand_weight[1]], axis=1))
    fresh = []
    for r in range(2):
        candidate = jnp.tanh(both[:, r * LANES : (r + 1) * LANES] + cand_bias[...])
        fresh.append(((1.0 - keep[r]) * hid[r] + keep[r] * candidate).reshape(EDGES, WIDTH, LANES))
    new_hidden[...] = jnp.concatenate(fresh, axis=1).astype(bf16)
    for e in range(EDGES):
        head = lax.dot_general(
            head_weight[...], new_hidden[e], (((1,), (1,)), ((), ())), preferred_element_type=f32
        )
        for h in range(4):
            heads[h, e : e + 1, :PIXELS] = head[h : h + 1]
    delta_u = heads[0, :EDGES, :PIXELS] + head_bias[0]
    delta_v = heads[1, :EDGES, :PIXELS] + head_bias[1]
    weight_u = sigmoid(heads[2, :EDGES, :PIXELS] + head_bias[2])
    weight_v = sigmoid(heads[3, :EDGES, :PIXELS] + head_bias[3])
    for h, value in enumerate((delta_u, delta_v, weight_u, weight_v)):
        revision[:, h, :] = value

    d = sources[:EDGES, :PIXELS]
    x = (pixel_col - (WIDTH - 1) / 2.0) / 40.0
    y = (pixel_row - (HEIGHT - 1) / 2.0) / 40.0
    depth_u = shift_x - x * shift_z
    depth_v = shift_y - y * shift_z
    resid_u = (grid_col - (WIDTH - 1) / 2.0) / 40.0 + delta_u - (x + d * depth_u)
    resid_v = (grid_row - (HEIGHT - 1) / 2.0) / 40.0 + delta_v - (y + d * depth_v)
    jac_u = (d, None, -x * d, -x * y, 1.0 + x * x, -y)
    jac_v = (None, d, -y * d, -(1.0 + y * y), x * y, x)
    wu, wv = weight_u * valid, weight_v * valid
    wide = lax.broadcasted_iota(jnp.int32, (EDGES, LANES), 1)
    sums = jnp.zeros((EDGES, LANES), f32)
    zero = jnp.zeros_like(d)

    def both_terms(a, u, v):
        left = zero if jac_u[a] is None or u is None else jac_u[a] * u
        right = zero if jac_v[a] is None or v is None else jac_v[a] * v
        return left + right

    def put(total, value, *where):
        value = jnp.sum(value, axis=1, keepdims=True)
        for k in where:
            total = jnp.where(wide == k, value, total)
        return total

    for a in range(6):
        u = None if jac_u[a] is None else jac_u[a] * wu
        v = None if jac_v[a] is None else jac_v[a] * wv
        for b in range(a, 6):
            sums = put(sums, both_terms(b, u, v), 6 * a + b, 6 * b + a)
        sums = put(sums, both_terms(a, wu * resid_u, wv * resid_v), 36 + a)
        depth_pose[:, a, :] = both_terms(a, wu * depth_u, wv * depth_v)
    pose[...] = sums
    curvature = wu * depth_u * depth_u + wv * depth_v * depth_v
    slope = wu * depth_u * resid_u + wv * depth_v * resid_v
    for n, value in enumerate((curvature, slope)):
        for i in range(KEYFRAMES):
            extra = jnp.where(loop_source == i, value[NEAR:], 0.0)
            depth_diagonal[i, n : n + 1, :] = (
                jnp.sum(value[4 * i : 4 * i + 4], axis=0, keepdims=True) + extra
            )


def on_device(tm_count, sub_count, feature_maps, context_maps, hidden_state, lookup_grid, loop_edges,
              inverse_depth, translations, update_reset_weight, update_reset_bias, candidate_weight,
              candidate_bias, correlation_weight, flow_weight, motion_bias, head_weight, head_bias):
    tm, sub = lax.axis_index("tm"), lax.axis_index("sub")
    first = (tm * sub_count + sub) * KEYFRAMES
    frame_total = tm_count * sub_count * KEYFRAMES
    channels = feature_maps.shape[-1]
    queries = feature_maps[:, :QUERY_ROWS].reshape(KEYFRAMES, PIXELS, channels)
    grid = lookup_grid.reshape(EDGES, PIXELS)
    wide = jnp.pad(grid, ((0, 0), (0, LANES - PIXELS)))
    high, low = (wide // WIDTH).astype(bf16), (wide % WIDTH).astype(bf16)

    def message(low_frame, edges):
        facts = [row for e, _, _ in edges for row in (high[e], low[e])]
        facts += [jnp.zeros((LANES,), bf16)] * (16 - len(facts))
        q = queries[low_frame : low_frame + 2].reshape(2 * PIXELS, channels)
        return jnp.concatenate([q, jnp.stack(facts)], axis=0)

    target = loop_edges[0, 1]
    target_block = target // KEYFRAMES
    numbers = (target_block // sub_count, target_block % sub_count, target % KEYFRAMES, tm, sub, 1)
    facts = [high[NEAR], low[NEAR]]
    facts += [jnp.full((LANES,), n).astype(bf16) for n in numbers]
    facts += [jnp.zeros((LANES,), bf16)] * (16 - len(facts))
    loop_query = lax.dynamic_index_in_dim(queries, loop_edges[0, 0] - first, 0, keepdims=False)
    loop_message = jnp.concatenate([loop_query, jnp.stack(facts)], axis=0)
    to_prev, to_next = message(0, TO_PREV), message(2, TO_NEXT)

    shape = jax.ShapeDtypeStruct
    whole = pl.BlockSpec(memory_space=VMEM)
    scalar = pl.BlockSpec(memory_space=pltpu.SMEM)
    dma = pltpu.SemaphoreType.DMA
    near_msg = (QUERY_MSG, LANES)
    loop_msg = (LOOP_MSG, LANES)
    from_prev, from_next, chosen = pl.pallas_call(
        functools.partial(queries_out, tm_count, sub_count),
        out_shape=(shape(near_msg, bf16), shape(near_msg, bf16), shape((LOOP_MOST,) + loop_msg, bf16)),
        in_specs=[whole] * 3,
        out_specs=(whole,) * 3,
        scratch_shapes=[
            VMEM(near_msg, bf16), VMEM(near_msg, bf16), VMEM((tm_count,) + loop_msg, bf16),
            VMEM((sub_count, LOOP_MOST) + loop_msg, bf16), VMEM((sub_count, LOOP_MOST) + loop_msg, bf16),
            dma((2, 2)), dma((2, tm_count)), dma((2, sub_count)),
        ],
        compiler_params=params(0),
        name="queries_out",
    )(to_prev, to_next, loop_message)

    tap_shape = (16, LANES)
    near, res_prev, res_next, loops = pl.pallas_call(
        correlate,
        out_shape=tuple(shape((n,) + tap_shape, f32) for n in (NEAR, 3, 3, LOOP_MOST)),
        in_specs=[whole] * 6,
        out_specs=(whole,) * 4,
        compiler_params=params(),
        name="correlate",
    )(feature_maps.reshape(KEYFRAMES, FRAME_PIXELS, channels), queries, grid, from_prev, from_next, chosen)

    near_prev, near_next, loop_corr = pl.pallas_call(
        functools.partial(results_back, tm_count, sub_count),
        out_shape=(shape((3,) + tap_shape, f32), shape((3,) + tap_shape, f32), shape(tap_shape, f32)),
        in_specs=[whole] * 3,
        out_specs=(whole,) * 3,
        scratch_shapes=[
            VMEM((3,) + tap_shape, f32), VMEM((3,) + tap_shape, f32),
            VMEM((sub_count, LOOP_MOST) + tap_shape, f32),
            VMEM((tm_count,) + tap_shape, f32), VMEM((tm_count,) + tap_shape, f32),
            dma((2, 2)), dma((2, tm_count)), dma((2, sub_count)),
        ],
        compiler_params=params(1),
        name="results_back",
    )(res_next, res_prev, loops)

    enc_weight = jnp.concatenate(
        [correlation_weight, flow_weight, motion_bias[None], jnp.zeros((4, LANES), f32)], axis=0
    )
    head_rows = jnp.concatenate([head_weight.T, jnp.zeros((12, LANES), bf16)], axis=0)
    correlation, new_hidden, revision, pose, depth_pose, depth_diagonal = pl.pallas_call(
        functools.partial(update, frame_total),
        out_shape=(
            shape((EDGES, TAPS, PIXELS), f32), shape((EDGES, PIXELS, LANES), bf16),
            shape((EDGES, 4, PIXELS), f32), shape((EDGES, LANES), f32),
            shape((EDGES, 6, PIXELS), f32), shape((KEYFRAMES, 2, PIXELS), f32),
        ),
        in_specs=[whole] * 8 + [scalar] * 3 + [whole] * 6 + [scalar],
        out_specs=(whole,) * 6,
        scratch_shapes=[
            VMEM((2, EDGES * WIDTH, 6 * LANES), bf16), VMEM((EDGES, PIXELS, LANES), f32),
            VMEM((4, 24, LANES), f32), VMEM((24, LANES), f32), VMEM((4, 24, LANES), f32),
        ],
        compiler_params=params(),
        name="update",
    )(
        near, near_prev, near_next, loop_corr, hidden_state.reshape(EDGES, PIXELS, LANES),
        context_maps.reshape(KEYFRAMES, PIXELS, LANES), grid, inverse_depth.reshape(KEYFRAMES, PIXELS),
        translations, loop_edges, first[None],
        update_reset_weight.reshape(3, 6 * LANES, 2 * LANES), update_reset_bias[None],
        candidate_weight.reshape(3, 6 * LANES, LANES), candidate_bias[None], enc_weight, head_rows, head_bias,
    )
    split = lambda a: a.reshape(a.shape[:-1] + (QUERY_ROWS, WIDTH))
    return (
        split(correlation), new_hidden.reshape(hidden_state.shape), split(revision),
        pose[:, :36].reshape(EDGES, 6, 6), pose[:, 36:42], split(depth_pose), split(depth_diagonal),
    )


def solution(mesh):
    lead = ("tm", "sub")
    over = lambda rank: P(lead, *([None] * (rank - 1)))
    in_specs = tuple(over(rank) for rank in (4, 4, 4, 3, 2, 3)) + (P(),) * 10
    out_specs = tuple(over(rank) for rank in (4, 4, 4, 3, 2, 4, 4))
    return jax.shard_map(
        functools.partial(on_device, mesh.shape["tm"], mesh.shape["sub"]),
        mesh=mesh, in_specs=in_specs, out_specs=out_specs, check_vma=False,
    )
```

```python
import functools
import math

import jax
import jax.numpy as jnp
from jax import lax
from jax.experimental import pallas as pl
from jax.experimental.pallas import tpu as pltpu
from jax.sharding import PartitionSpec as P

HEIGHT = 30
WIDTH = 40
KEYFRAMES = 4
QUERY_ROWS = 2
LOOP_MOST = 4
PIXELS = QUERY_ROWS * WIDTH
FRAME_PIXELS = HEIGHT * WIDTH
NEAR = 4 * KEYFRAMES
EDGES = NEAR + 1
LANES = 128
TAPS = 9
MESH = pl.DeviceIdType.MESH
VMEM = pltpu.VMEM
bf16 = jnp.bfloat16
f32 = jnp.float32
highest = lax.Precision.HIGHEST
neighbour_steps = (-2, -1, 1, 2)

TO_PREV = ((0, 0, 2), (1, 0, 3), (4, 1, 3))
TO_NEXT = ((11, 2, 0), (14, 3, 0), (15, 3, 1))
QUERY_MSG = 2 * PIXELS + 16
LOOP_MSG = PIXELS + 16


def params(collective_id=None):
    return pltpu.CompilerParams(
        collective_id=collective_id,
        has_side_effects=collective_id is not None,
        vmem_limit_bytes=48 * 1024 * 1024,
    )


def places(tm_count, sub_count):
    tm, sub = lax.axis_index("tm"), lax.axis_index("sub")
    block = tm * sub_count + sub
    total = tm_count * sub_count
    after = lax.rem(block + 1, total)
    before = lax.rem(block + total - 1, total)
    coords = lambda b: (b // sub_count, lax.rem(b, sub_count))
    line = [(lax.rem(tm + d, tm_count), sub) for d in range(1, tm_count)]
    column = [(tm, lax.rem(sub + d, sub_count)) for d in range(1, sub_count)]
    return tm, sub, coords(before), coords(after), line, column


def greet(peers):
    barrier = pltpu.get_barrier_semaphore()
    for peer in peers:
        pl.semaphore_signal(barrier, inc=1, device_id=peer, device_id_type=MESH)
    pl.semaphore_wait(barrier, len(peers))


def send(src, dst, send_sem, recv_sem, peer):
    copy = pltpu.make_async_remote_copy(
        src_ref=src, dst_ref=dst, send_sem=send_sem, recv_sem=recv_sem,
        device_id=peer, device_id_type=MESH,
    )
    copy.start()
    return copy


def flatten(x):
    tail = jnp.zeros((x.shape[0], LANES - PIXELS), x.dtype)
    return jnp.concatenate([x[:, 0, :], x[:, 1, :], tail], axis=1)


def split_rows(grid):
    flat = flatten(grid).astype(f32)
    high = jnp.floor((flat + 0.5) * (1.0 / WIDTH))
    return flat, high, flat - float(WIDTH) * high


def queries_out(tm_count, sub_count, features, grid, ends, from_prev, from_next, chosen,
                to_prev, to_next, got_prev, got_next, line, near_sem, sub_sem, line_sem, pair_sem):
    tm, sub, before, after, _, column = places(tm_count, sub_count)
    half = tm_count // 2
    line_peers = [(lax.rem(tm + 2 * d, tm_count), sub) for d in range(1, half)]
    other = (tm + 1 - 2 * lax.rem(tm, 2), sub)
    peers = [before, after, other] + line_peers + column
    barrier = pltpu.get_barrier_semaphore()
    for peer in peers:
        pl.semaphore_signal(barrier, inc=1, device_id=peer, device_id_type=MESH)

    _, high, low = split_rows(grid)
    query = lambda i: features[i].astype(f32).reshape(PIXELS, LANES)

    def facts(rows):
        return jnp.concatenate(rows + [jnp.zeros((16 - len(rows), LANES), f32)], axis=0)

    target = ends[0, 1]
    target_block = target // KEYFRAMES
    numbers = (
        target_block // sub_count, lax.rem(target_block, sub_count), lax.rem(target, KEYFRAMES), tm, sub
    )
    rows = [high[NEAR:], low[NEAR:]] + [jnp.full((1, LANES), n.astype(f32)) for n in numbers]
    rows += [jnp.ones((1, LANES), f32)]
    line[0, 0, 0, :PIXELS] = query(lax.rem(ends[0, 0], KEYFRAMES)).astype(bf16)
    line[0, 0, 0, PIXELS:] = facts(rows).astype(bf16)
    for out, start, edges in ((to_prev, 0, TO_PREV), (to_next, 2, TO_NEXT)):
        for n in range(2):
            out[n * PIXELS : (n + 1) * PIXELS] = query(start + n).astype(bf16)
        rows = [row for e, _, _ in edges for row in (high[e : e + 1], low[e : e + 1])]
        out[2 * PIXELS :] = facts(rows).astype(bf16)

    pl.semaphore_wait(barrier, len(peers))
    sub_copies = [
        send(line.at[0, 0, 0], line.at[0, 0, e + 1], sub_sem.at[0, e], sub_sem.at[1, e], peer)
        for e, peer in enumerate(column)
    ]
    near_copies = [
        send(to_next, got_prev, near_sem.at[0, 0], near_sem.at[1, 0], after),
        send(to_prev, got_next, near_sem.at[0, 1], near_sem.at[1, 1], before),
    ]
    for copy in sub_copies:
        copy.wait()
    line_copies = [
        send(line.at[0, 0], line.at[0, d + 1], line_sem.at[0, d], line_sem.at[1, d], peer)
        for d, peer in enumerate(line_peers)
    ]
    pair_copies = [send(line.at[0, 0], line.at[1, 0], pair_sem.at[0, 0], pair_sem.at[1, 0], other)]
    chosen[...] = jnp.zeros_like(chosen)
    here, own = tm.astype(f32), sub.astype(f32)

    def take_from(side, d, count):
        for e in range(sub_count):
            message = line[side, d, e]
            about = message[PIXELS:].astype(f32)
            match = ((about[2:3] == here) & (about[3:4] == own)).astype(f32)
            for m in range(LOOP_MOST):
                take = jnp.where(count == float(m), match, 0.0).astype(bf16)
                chosen[m] += message * take
            count = count + match
        return count

    count = take_from(0, 0, jnp.zeros((1, LANES), f32))
    for d in range(1, half):
        line_copies[d - 1].wait()
        pair_copies.append(
            send(line.at[0, d], line.at[1, d], pair_sem.at[0, d], pair_sem.at[1, d], other)
        )
        count = take_from(0, d, count)
    for copy in near_copies:
        copy.wait()
    from_prev[...] = got_prev[...]
    from_next[...] = got_next[...]
    for d in range(half):
        pair_copies[d].wait()
        count = take_from(1, d, count)


def results_back(tm_count, sub_count, to_prev, to_next, loops, near_prev, near_next, loop_corr,
                 got_prev, got_next, pool, backs, lines, near_sem, line_sem, sub_sem):
    tm, sub, before, after, line_peers, column = places(tm_count, sub_count)
    greet([before, after] + line_peers + column)
    sub_copies = [
        send(loops, pool.at[e + 1], sub_sem.at[0, e], sub_sem.at[1, e], peer)
        for e, peer in enumerate(column)
    ]
    near_copies = [
        send(to_next, got_prev, near_sem.at[0, 0], near_sem.at[1, 0], after),
        send(to_prev, got_next, near_sem.at[0, 1], near_sem.at[1, 1], before),
    ]
    pool[0] = loops[...]
    own = sub.astype(f32)
    for copy in sub_copies:
        copy.wait()

    def pick(d, carry):
        wanted = lax.rem(tm + d, tm_count).astype(f32)
        total = jnp.zeros((16, LANES), f32)
        for e in range(sub_count):
            for k in range(LOOP_MOST):
                found = pool[e, k]
                match = (found[9:10] == wanted) & (found[10:11] == own)
                total = total + found * jnp.where(match, found[11:12], 0.0)
        backs[d] = total
        return carry

    lax.fori_loop(0, tm_count, pick, 0)
    line_copies = [
        send(backs.at[d + 1], lines.at[d + 1], line_sem.at[0, d], line_sem.at[1, d], peer)
        for d, peer in enumerate(line_peers)
    ]
    total = backs[0]
    for d, copy in enumerate(line_copies):
        copy.wait()
        total = total + lines[d + 1]
    loop_corr[...] = total
    for copy in near_copies:
        copy.wait()
    near_prev[...] = got_prev[...]
    near_next[...] = got_next[...]


def tap_steps(shape):
    k = lax.broadcasted_iota(jnp.int32, shape, 1)
    row = jnp.where(k >= 6, 1, jnp.where(k >= 3, 0, -1))
    step = row * WIDTH + (k - 3 * (row + 1) - 1)
    return jnp.where(k < TAPS, step, 0)


def correlate(features, heads, grid, from_prev, from_next, chosen, near, to_prev, to_next, loops):
    scale = 1.0 / math.sqrt(features.shape[-1])
    rows = lax.broadcasted_iota(jnp.int32, (16, LANES), 0)

    def split_grid(facts):
        return facts[0:1].astype(f32) * float(WIDTH) + facts[1:2].astype(f32)

    flat = flatten(grid).astype(f32)
    grids = [flat[e : e + 1] for e in range(NEAR)]
    queries = [heads[i].astype(f32).reshape(PIXELS, LANES).astype(bf16) for i in range(KEYFRAMES)]
    pairs = [[] for _ in range(KEYFRAMES)]
    for i in range(KEYFRAMES):
        for n, step in enumerate(neighbour_steps):
            if 0 <= i + step < KEYFRAMES:
                pairs[i + step].append((queries[i], grids[4 * i + n], near, 4 * i + n))
    for refs, edges, low, out in ((from_prev, TO_NEXT, 2, to_next), (from_next, TO_PREV, 0, to_prev)):
        for n, (_, source, target) in enumerate(edges):
            q = refs[(source - low) * PIXELS : (source - low + 1) * PIXELS]
            facts = refs[2 * PIXELS : 2 * PIXELS + 16].astype(f32)
            pairs[target].append((q, split_grid(facts[2 * n : 2 * n + 2]), out, n))

    def look_up(q, pixel_rows, frame):
        count = len(pixel_rows)
        stacked = jnp.concatenate(pixel_rows + [jnp.zeros((8 - count % 8, LANES), f32)], axis=0)
        columns = jnp.transpose(stacked)
        index = jnp.concatenate(
            [
                jnp.broadcast_to(columns[:PIXELS, n : n + 1], (PIXELS, LANES)).astype(jnp.int32)
                for n in range(count)
            ],
            axis=0,
        )
        index = index + tap_steps(index.shape)
        found = jnp.zeros(index.shape, f32)
        for start in range(0, FRAME_PIXELS, LANES):
            base = min(start, FRAME_PIXELS - LANES)
            part = frame[pl.ds(base, LANES), :]
            volume = lax.dot_general(q, part, (((1,), (1,)), ((), ())), preferred_element_type=f32)
            local = index - base
            inside = (index >= start) & (index < start + LANES)
            picked = jnp.take_along_axis(volume, local & (LANES - 1), axis=1)
            found = jnp.where(inside, picked, found)
        found = found * scale
        return [jnp.transpose(found[n * PIXELS : (n + 1) * PIXELS])[:16] for n in range(count)]

    for j in range(KEYFRAMES):
        q = jnp.concatenate([p[0] for p in pairs[j]], axis=0)
        pixel_rows = [p[1] for p in pairs[j]]
        for result, (_, _, out, n) in zip(look_up(q, pixel_rows, features.at[j]), pairs[j]):
            out[n, :, :PIXELS] = result
            out[n, :, PIXELS:] = jnp.zeros((16, LANES - PIXELS), f32)

    for k in range(LOOP_MOST):
        facts = chosen[k, PIXELS:].astype(f32)
        frame = jnp.max(facts[4:5]).astype(jnp.int32)
        (result,) = look_up(chosen[k, :PIXELS], [split_grid(facts[0:2])], features.at[frame])
        result = jnp.concatenate([result, jnp.zeros((16, LANES - PIXELS), f32)], axis=1)
        for row, fact in ((9, 5), (10, 6), (11, 7)):
            result = jnp.where(rows == row, jnp.broadcast_to(facts[fact : fact + 1], (16, LANES)), result)
        loops[k] = result


def sigmoid(x):
    return 0.5 * jnp.tanh(0.5 * x) + 0.5


def update(tm_count, sub_count, near, near_prev, near_next, loop_corr, hidden, context, grid, depth, moves, ends,
           gate_weight, gate_bias, cand_weight, cand_bias, corr_weight, flow_weight, motion_bias, head_weight, head_bias,
           correlation, new_hidden, revision, pose, gradient, depth_pose, depth_diagonal,
           taps, inputs, heads, sources, shifts, enc_weight):
    frame_total = tm_count * sub_count * KEYFRAMES
    first = (lax.axis_index("tm") * sub_count + lax.axis_index("sub")) * KEYFRAMES
    enc_weight[0:TAPS] = corr_weight[...]
    enc_weight[TAPS : TAPS + 2] = flow_weight[...]
    enc_weight[TAPS + 2 : TAPS + 3] = motion_bias[...]
    enc_weight[TAPS + 3 :] = jnp.zeros((16 - TAPS - 3, LANES), f32)
    head_rows = jnp.transpose(head_weight[...].astype(f32))
    head_rows = jnp.concatenate([head_rows, jnp.zeros((12, LANES), f32)], axis=0).astype(bf16)
    loop_source = lax.rem(ends[0, 0], KEYFRAMES)
    targets, valids = [], []
    for e in range(EDGES):
        if e < NEAR:
            source = first + e // 4
            target = first + e // 4 + neighbour_steps[e % 4]
        else:
            source, target = ends[0, 0], ends[0, 1]
        ok = jnp.where((target >= 0) & (target < frame_total), 1.0, 0.0).astype(f32)
        safe = jnp.clip(target, 0, frame_total - 1)
        for a in range(3):
            shifts[a, e : e + 1, :] = jnp.full((1, LANES), moves[a, safe] - moves[a, source], f32)
        shifts[3, e : e + 1, :] = jnp.full((1, LANES), ok, f32)
        valids.append(ok)
    shift_x, shift_y, shift_z, valid = [shifts[a, :EDGES, :PIXELS] for a in range(4)]

    lane = lax.broadcasted_iota(jnp.int32, (EDGES, PIXELS), 1)
    pixel_row = jnp.where(lane >= WIDTH, 1, 0)
    pixel_col = (lane - WIDTH * pixel_row).astype(f32)
    pixel_row = pixel_row.astype(f32)
    _, grid_row, grid_col = [value[:, :PIXELS] for value in split_rows(grid)]
    flow_u = (grid_col - pixel_col) / 40.0
    flow_v = (grid_row - pixel_row) / 40.0

    crossing = {e: near_next[n] for n, (e, _, _) in enumerate(TO_NEXT)}
    crossing.update({e: near_prev[n] for n, (e, _, _) in enumerate(TO_PREV)})
    low = lax.broadcasted_iota(jnp.int32, (16, PIXELS), 0)
    for e in range(EDGES):
        found = loop_corr[...] if e == NEAR else crossing[e] if e in crossing else near[e]
        found = found[:, :PIXELS] * valids[e]
        correlation[e, :, 0, :] = found[:TAPS, :WIDTH]
        correlation[e, :, 1, :] = found[:TAPS, WIDTH:]
        rows = jnp.where(low < TAPS, found, 0.0)
        rows = jnp.where(low == 9, jnp.broadcast_to(flow_u[e : e + 1], rows.shape), rows)
        rows = jnp.where(low == 10, jnp.broadcast_to(flow_v[e : e + 1], rows.shape), rows)
        rows = jnp.where(low == 11, 1.0, rows)
        motion = lax.dot_general(
            rows, enc_weight[...], (((0,), (0,)), ((), ())), precision=highest, preferred_element_type=f32
        )
        about = context[e // 4 if e < NEAR else loop_source].astype(f32)
        inputs[e] = (jax.nn.relu(motion) + about).astype(bf16).astype(f32)
        sources[e : e + 1] = flatten(depth[pl.ds(e // 4 if e < NEAR else loop_source, 1)])

    def halves(x):
        return x[:, :WIDTH].reshape(-1, LANES), x[:, WIDTH:].reshape(-1, LANES)

    count = EDGES * WIDTH
    col = lax.broadcasted_iota(jnp.int32, (EDGES, WIDTH, LANES), 1).reshape(count, LANES)

    def around(x):
        left = jnp.where(col == 0, 0.0, pltpu.roll(x, 1, 0))
        right = jnp.where(col == WIDTH - 1, 0.0, pltpu.roll(x, count - 1, 0))
        return left.astype(bf16), x.astype(bf16), right.astype(bf16)

    hid = halves(hidden[...].astype(f32))
    inp = halves(inputs[...])
    for r in range(2):
        for b, value in enumerate(around(hid[r])):
            taps[r, :, 2 * b * LANES : (2 * b + 1) * LANES] = value
        for b, value in enumerate(around(inp[r])):
            taps[r, :, (2 * b + 1) * LANES : (2 * b + 2) * LANES] = value
    dot = functools.partial(jnp.dot, preferred_element_type=f32)
    keep = []
    gated = []
    for r in range(2):
        gates = dot(taps[0], gate_weight[1 - r]) + dot(taps[1], gate_weight[2 - r]) + gate_bias[...]
        gates = sigmoid(gates)
        keep.append(gates[:, :LANES])
        gated.append((gates[:, LANES:] * hid[r]).astype(bf16).astype(f32))
    for r in range(2):
        for b, value in enumerate(around(gated[r])):
            taps[r, :, 2 * b * LANES : (2 * b + 1) * LANES] = value
    both = dot(taps[0], jnp.concatenate([cand_weight[1], cand_weight[0]], axis=1))
    both = both + dot(taps[1], jnp.concatenate([cand_weight[2], cand_weight[1]], axis=1))
    fresh = []
    for r in range(2):
        candidate = jnp.tanh(both[:, r * LANES : (r + 1) * LANES] + cand_bias[...])
        fresh.append(((1.0 - keep[r]) * hid[r] + keep[r] * candidate).reshape(EDGES, WIDTH, LANES))
    new_hidden[...] = jnp.concatenate(fresh, axis=1).astype(bf16)
    for e in range(EDGES):
        head = lax.dot_general(
            head_rows, new_hidden[e], (((1,), (1,)), ((), ())), preferred_element_type=f32
        )
        for h in range(4):
            heads[h, e : e + 1, :PIXELS] = head[h : h + 1]
    delta_u = heads[0, :EDGES, :PIXELS] + head_bias[0]
    delta_v = heads[1, :EDGES, :PIXELS] + head_bias[1]
    weight_u = sigmoid(heads[2, :EDGES, :PIXELS] + head_bias[2])
    weight_v = sigmoid(heads[3, :EDGES, :PIXELS] + head_bias[3])
    def halve(out, n, value):
        out[:, n, 0, :] = value[:, :WIDTH]
        out[:, n, 1, :] = value[:, WIDTH:]

    for h, value in enumerate((delta_u, delta_v, weight_u, weight_v)):
        halve(revision, h, value)

    d = sources[:EDGES, :PIXELS]
    x = (pixel_col - (WIDTH - 1) / 2.0) / 40.0
    y = (pixel_row - (HEIGHT - 1) / 2.0) / 40.0
    depth_u = shift_x - x * shift_z
    depth_v = shift_y - y * shift_z
    resid_u = (grid_col - (WIDTH - 1) / 2.0) / 40.0 + delta_u - (x + d * depth_u)
    resid_v = (grid_row - (HEIGHT - 1) / 2.0) / 40.0 + delta_v - (y + d * depth_v)
    jac_u = (d, None, -x * d, -x * y, 1.0 + x * x, -y)
    jac_v = (None, d, -y * d, -(1.0 + y * y), x * y, x)
    wu, wv = weight_u * valid, weight_v * valid
    six = lax.broadcasted_iota(jnp.int32, (EDGES, 6), 1)
    blocks = [jnp.zeros((EDGES, 6), f32)] * 6
    slopes = jnp.zeros((EDGES, 6), f32)
    zero = jnp.zeros_like(d)

    def both_terms(a, u, v):
        left = zero if jac_u[a] is None or u is None else jac_u[a] * u
        right = zero if jac_v[a] is None or v is None else jac_v[a] * v
        return left + right

    def put(total, value, k):
        return jnp.where(six == k, value, total)

    for a in range(6):
        u = None if jac_u[a] is None else jac_u[a] * wu
        v = None if jac_v[a] is None else jac_v[a] * wv
        for b in range(a, 6):
            value = jnp.sum(both_terms(b, u, v), axis=1, keepdims=True)
            blocks[a] = put(blocks[a], value, b)
            if b > a:
                blocks[b] = put(blocks[b], value, a)
        value = jnp.sum(both_terms(a, wu * resid_u, wv * resid_v), axis=1, keepdims=True)
        slopes = put(slopes, value, a)
        halve(depth_pose, a, both_terms(a, wu * depth_u, wv * depth_v))
    for a in range(6):
        pose[:, a, :] = blocks[a]
    gradient[...] = slopes
    curvature = wu * depth_u * depth_u + wv * depth_v * depth_v
    slope = wu * depth_u * resid_u + wv * depth_v * resid_v
    for n, value in enumerate((curvature, slope)):
        for i in range(KEYFRAMES):
            extra = jnp.where(loop_source == i, value[NEAR:], 0.0)
            extra = extra + jnp.sum(value[4 * i : 4 * i + 4], axis=0, keepdims=True)
            depth_diagonal[i, n, 0:1, :] = extra[:, :WIDTH]
            depth_diagonal[i, n, 1:2, :] = extra[:, WIDTH:]


def on_device(tm_count, sub_count, feature_maps, context_maps, hidden_state, lookup_grid, loop_edges,
              inverse_depth, translations, update_reset_weight, update_reset_bias, candidate_weight,
              candidate_bias, correlation_weight, flow_weight, motion_bias, head_weight, head_bias):
    channels = feature_maps.shape[-1]
    shape = jax.ShapeDtypeStruct
    whole = pl.BlockSpec(memory_space=VMEM)
    scalar = pl.BlockSpec(memory_space=pltpu.SMEM)
    dma = pltpu.SemaphoreType.DMA
    near_msg = (QUERY_MSG, LANES)
    loop_msg = (LOOP_MSG, LANES)
    half = tm_count // 2
    heads_spec = pl.BlockSpec(
        (KEYFRAMES, QUERY_ROWS, WIDTH, channels), lambda i: (0, 0, 0, 0), memory_space=VMEM
    )
    from_prev, from_next, chosen = pl.pallas_call(
        functools.partial(queries_out, tm_count, sub_count),
        grid=(1,),
        out_shape=(shape(near_msg, bf16), shape(near_msg, bf16), shape((LOOP_MOST,) + loop_msg, bf16)),
        in_specs=[heads_spec, whole, scalar],
        out_specs=(whole,) * 3,
        scratch_shapes=[VMEM(near_msg, bf16)] * 4 + [
            VMEM((2, half, sub_count) + loop_msg, bf16),
            dma((2, 2)), dma((2, sub_count)), dma((2, half)), dma((2, half)),
        ],
        compiler_params=params(0),
        name="queries_out",
    )(feature_maps, lookup_grid, loop_edges)

    tap_shape = (16, LANES)
    near, res_prev, res_next, loops = pl.pallas_call(
        correlate,
        grid=(1,),
        out_shape=tuple(shape((n,) + tap_shape, f32) for n in (NEAR, 3, 3, LOOP_MOST)),
        in_specs=[whole, heads_spec] + [whole] * 4,
        out_specs=(whole,) * 4,
        compiler_params=params(),
        name="correlate",
    )(feature_maps.reshape(KEYFRAMES, FRAME_PIXELS, channels), feature_maps, lookup_grid, from_prev, from_next, chosen)

    near_prev, near_next, loop_corr = pl.pallas_call(
        functools.partial(results_back, tm_count, sub_count),
        out_shape=(shape((3,) + tap_shape, f32), shape((3,) + tap_shape, f32), shape(tap_shape, f32)),
        in_specs=[whole] * 3,
        out_specs=(whole,) * 3,
        scratch_shapes=[
            VMEM((3,) + tap_shape, f32), VMEM((3,) + tap_shape, f32),
            VMEM((sub_count, LOOP_MOST) + tap_shape, f32),
            VMEM((tm_count,) + tap_shape, f32), VMEM((tm_count,) + tap_shape, f32),
            dma((2, 2)), dma((2, tm_count)), dma((2, sub_count)),
        ],
        compiler_params=params(1),
        name="results_back",
    )(res_next, res_prev, loops)

    correlation, new_hidden, revision, pose, gradient, depth_pose, depth_diagonal = pl.pallas_call(
        functools.partial(update, tm_count, sub_count),
        out_shape=(
            shape((EDGES, TAPS, QUERY_ROWS, WIDTH), f32), shape((EDGES, PIXELS, LANES), bf16),
            shape((EDGES, 4, QUERY_ROWS, WIDTH), f32), shape((EDGES, 6, 6), f32), shape((EDGES, 6), f32),
            shape((EDGES, 6, QUERY_ROWS, WIDTH), f32), shape((KEYFRAMES, 2, QUERY_ROWS, WIDTH), f32),
        ),
        in_specs=[whole] * 8 + [scalar] * 2 + [whole] * 8 + [scalar],
        out_specs=(whole,) * 7,
        scratch_shapes=[
            VMEM((2, EDGES * WIDTH, 6 * LANES), bf16), VMEM((EDGES, PIXELS, LANES), f32),
            VMEM((4, 24, LANES), f32), VMEM((24, LANES), f32), VMEM((4, 24, LANES), f32), VMEM((16, LANES), f32),
        ],
        compiler_params=params(),
        name="update",
    )(
        near, near_prev, near_next, loop_corr, hidden_state.reshape(EDGES, PIXELS, LANES),
        context_maps.reshape(KEYFRAMES, PIXELS, LANES), lookup_grid, inverse_depth, translations, loop_edges,
        update_reset_weight.reshape(3, 6 * LANES, 2 * LANES), update_reset_bias[None],
        candidate_weight.reshape(3, 6 * LANES, LANES), candidate_bias[None], correlation_weight, flow_weight,
        motion_bias[None], head_weight, head_bias,
    )
    return (
        correlation, new_hidden.reshape(hidden_state.shape), revision, pose, gradient, depth_pose, depth_diagonal
    )


def solution(mesh):
    lead = ("tm", "sub")
    over = lambda rank: P(lead, *([None] * (rank - 1)))
    in_specs = tuple(over(rank) for rank in (4, 4, 4, 3, 2, 3)) + (P(),) * 10
    out_specs = tuple(over(rank) for rank in (4, 4, 4, 3, 2, 4, 4))
    return jax.shard_map(
        functools.partial(on_device, mesh.shape["tm"], mesh.shape["sub"]),
        mesh=mesh, in_specs=in_specs, out_specs=out_specs, check_vma=False,
    )
```

```python
import functools
import math

import jax
import jax.numpy as jnp
from jax import lax
from jax.experimental import pallas as pl
from jax.experimental.pallas import tpu as pltpu
from jax.sharding import PartitionSpec as P

HEIGHT = 30
WIDTH = 40
KEYFRAMES = 4
QUERY_ROWS = 2
LOOP_MOST = 4
PIXELS = QUERY_ROWS * WIDTH
FRAME_PIXELS = HEIGHT * WIDTH
NEAR = 4 * KEYFRAMES
EDGES = NEAR + 1
LANES = 128
TAPS = 9
MESH = pl.DeviceIdType.MESH
VMEM = pltpu.VMEM
bf16 = jnp.bfloat16
f32 = jnp.float32
highest = lax.Precision.HIGHEST
neighbour_steps = (-2, -1, 1, 2)

TO_PREV = ((0, 0, 2), (1, 0, 3), (4, 1, 3))
TO_NEXT = ((11, 2, 0), (14, 3, 0), (15, 3, 1))
QUERY_MSG = 2 * PIXELS + 16
LOOP_MSG = PIXELS + 16


def params(collective_id=None):
    return pltpu.CompilerParams(
        collective_id=collective_id,
        has_side_effects=collective_id is not None,
        vmem_limit_bytes=48 * 1024 * 1024,
    )


def places(tm_count, sub_count):
    tm, sub = lax.axis_index("tm"), lax.axis_index("sub")
    block = tm * sub_count + sub
    total = tm_count * sub_count
    after = lax.rem(block + 1, total)
    before = lax.rem(block + total - 1, total)
    coords = lambda b: (b // sub_count, lax.rem(b, sub_count))
    line = [(lax.rem(tm + d, tm_count), sub) for d in range(1, tm_count)]
    column = [(tm, lax.rem(sub + d, sub_count)) for d in range(1, sub_count)]
    return tm, sub, coords(before), coords(after), line, column


def greet(peers):
    barrier = pltpu.get_barrier_semaphore()
    for peer in peers:
        pl.semaphore_signal(barrier, inc=1, device_id=peer, device_id_type=MESH)
    pl.semaphore_wait(barrier, len(peers))


def send(src, dst, send_sem, recv_sem, peer):
    copy = pltpu.make_async_remote_copy(
        src_ref=src, dst_ref=dst, send_sem=send_sem, recv_sem=recv_sem,
        device_id=peer, device_id_type=MESH,
    )
    copy.start()
    return copy


def flatten(x):
    tail = jnp.zeros((x.shape[0], LANES - PIXELS), x.dtype)
    return jnp.concatenate([x[:, 0, :], x[:, 1, :], tail], axis=1)


def split_rows(grid):
    flat = flatten(grid).astype(f32)
    high = jnp.floor((flat + 0.5) * (1.0 / WIDTH))
    return flat, high, flat - float(WIDTH) * high


def queries_out(tm_count, sub_count, features, grid, ends, from_prev, from_next, chosen,
                to_prev, to_next, got_prev, got_next, line, near_sem, sub_sem, line_sem, pair_sem):
    tm, sub, before, after, _, column = places(tm_count, sub_count)
    half = tm_count // 2
    line_peers = [(lax.rem(tm + 2 * d, tm_count), sub) for d in range(1, half)]
    other = (tm + 1 - 2 * lax.rem(tm, 2), sub)
    peers = [before, after, other] + line_peers + column
    barrier = pltpu.get_barrier_semaphore()
    for peer in peers:
        pl.semaphore_signal(barrier, inc=1, device_id=peer, device_id_type=MESH)

    _, high, low = split_rows(grid)
    query = lambda i: features[i].astype(f32).reshape(PIXELS, LANES)

    def facts(rows):
        return jnp.concatenate(rows + [jnp.zeros((16 - len(rows), LANES), f32)], axis=0)

    target = ends[0, 1]
    target_block = target // KEYFRAMES
    numbers = (
        target_block // sub_count, lax.rem(target_block, sub_count), lax.rem(target, KEYFRAMES), tm, sub
    )
    rows = [high[NEAR:], low[NEAR:]] + [jnp.full((1, LANES), n.astype(f32)) for n in numbers]
    rows += [jnp.ones((1, LANES), f32)]
    line[0, 0, 0, :PIXELS] = query(lax.rem(ends[0, 0], KEYFRAMES)).astype(bf16)
    line[0, 0, 0, PIXELS:] = facts(rows).astype(bf16)
    for out, start, edges in ((to_prev, 0, TO_PREV), (to_next, 2, TO_NEXT)):
        for n in range(2):
            out[n * PIXELS : (n + 1) * PIXELS] = query(start + n).astype(bf16)
        rows = [row for e, _, _ in edges for row in (high[e : e + 1], low[e : e + 1])]
        out[2 * PIXELS :] = facts(rows).astype(bf16)

    pl.semaphore_wait(barrier, len(peers))
    sub_copies = [
        send(line.at[0, 0, 0], line.at[0, 0, e + 1], sub_sem.at[0, e], sub_sem.at[1, e], peer)
        for e, peer in enumerate(column)
    ]
    near_copies = [
        send(to_next, got_prev, near_sem.at[0, 0], near_sem.at[1, 0], after),
        send(to_prev, got_next, near_sem.at[0, 1], near_sem.at[1, 1], before),
    ]
    for copy in sub_copies:
        copy.wait()
    line_copies = [
        send(line.at[0, 0], line.at[0, d + 1], line_sem.at[0, d], line_sem.at[1, d], peer)
        for d, peer in enumerate(line_peers)
    ]
    pair_copies = [send(line.at[0, 0], line.at[1, 0], pair_sem.at[0, 0], pair_sem.at[1, 0], other)]
    chosen[...] = jnp.zeros_like(chosen)
    here, own = tm.astype(f32), sub.astype(f32)

    def take_from(side, d, count):
        for e in range(sub_count):
            message = line[side, d, e]
            about = message[PIXELS:].astype(f32)
            match = ((about[2:3] == here) & (about[3:4] == own)).astype(f32)
            for m in range(LOOP_MOST):
                take = jnp.where(count == float(m), match, 0.0).astype(bf16)
                chosen[m] += message * take
            count = count + match
        return count

    count = take_from(0, 0, jnp.zeros((1, LANES), f32))
    for d in range(1, half):
        line_copies[d - 1].wait()
        pair_copies.append(
            send(line.at[0, d], line.at[1, d], pair_sem.at[0, d], pair_sem.at[1, d], other)
        )
        count = take_from(0, d, count)
    for copy in near_copies:
        copy.wait()
    from_prev[...] = got_prev[...]
    from_next[...] = got_next[...]
    for d in range(half):
        pair_copies[d].wait()
        count = take_from(1, d, count)


def results_back(tm_count, sub_count, to_prev, to_next, loops, near_prev, near_next, loop_corr,
                 got_prev, got_next, pool, backs, lines, near_sem, line_sem, sub_sem):
    tm, sub, before, after, line_peers, column = places(tm_count, sub_count)
    greet([before, after] + line_peers + column)
    sub_copies = [
        send(loops, pool.at[e + 1], sub_sem.at[0, e], sub_sem.at[1, e], peer)
        for e, peer in enumerate(column)
    ]
    near_copies = [
        send(to_next, got_prev, near_sem.at[0, 0], near_sem.at[1, 0], after),
        send(to_prev, got_next, near_sem.at[0, 1], near_sem.at[1, 1], before),
    ]
    pool[0] = loops[...]
    own = sub.astype(f32)
    for copy in sub_copies:
        copy.wait()

    def pick(d, carry):
        wanted = lax.rem(tm + d, tm_count).astype(f32)
        total = jnp.zeros((16, LANES), f32)
        for e in range(sub_count):
            for k in range(LOOP_MOST):
                found = pool[e, k]
                match = (found[9:10] == wanted) & (found[10:11] == own)
                total = total + found * jnp.where(match, found[11:12], 0.0)
        backs[d] = total
        return carry

    lax.fori_loop(0, tm_count, pick, 0)
    line_copies = [
        send(backs.at[d + 1], lines.at[d + 1], line_sem.at[0, d], line_sem.at[1, d], peer)
        for d, peer in enumerate(line_peers)
    ]
    total = backs[0]
    for d, copy in enumerate(line_copies):
        copy.wait()
        total = total + lines[d + 1]
    loop_corr[...] = total
    for copy in near_copies:
        copy.wait()
    near_prev[...] = got_prev[...]
    near_next[...] = got_next[...]


def tap_steps(shape):
    k = lax.broadcasted_iota(jnp.int32, shape, 1)
    row = jnp.where(k >= 6, 1, jnp.where(k >= 3, 0, -1))
    step = row * WIDTH + (k - 3 * (row + 1) - 1)
    return jnp.where(k < TAPS, step, 0)


def correlate(features, heads, grid, from_prev, from_next, chosen, near, to_prev, to_next, loops):
    scale = 1.0 / math.sqrt(features.shape[-1])
    rows = lax.broadcasted_iota(jnp.int32, (16, LANES), 0)

    def split_grid(facts):
        return facts[0:1].astype(f32) * float(WIDTH) + facts[1:2].astype(f32)

    flat = flatten(grid).astype(f32)
    grids = [flat[e : e + 1] for e in range(NEAR)]
    queries = [heads[i].astype(f32).reshape(PIXELS, LANES).astype(bf16) for i in range(KEYFRAMES)]
    pairs = [[] for _ in range(KEYFRAMES)]
    for i in range(KEYFRAMES):
        for n, step in enumerate(neighbour_steps):
            if 0 <= i + step < KEYFRAMES:
                pairs[i + step].append((queries[i], grids[4 * i + n], near, 4 * i + n))
    for refs, edges, low, out in ((from_prev, TO_NEXT, 2, to_next), (from_next, TO_PREV, 0, to_prev)):
        for n, (_, source, target) in enumerate(edges):
            q = refs[(source - low) * PIXELS : (source - low + 1) * PIXELS]
            facts = refs[2 * PIXELS : 2 * PIXELS + 16].astype(f32)
            pairs[target].append((q, split_grid(facts[2 * n : 2 * n + 2]), out, n))

    def look_up(q, pixel_rows, frame):
        count = len(pixel_rows)
        stacked = jnp.concatenate(pixel_rows + [jnp.zeros((8 - count % 8, LANES), f32)], axis=0)
        columns = jnp.transpose(stacked)
        index = jnp.concatenate(
            [
                jnp.broadcast_to(columns[:PIXELS, n : n + 1], (PIXELS, LANES)).astype(jnp.int32)
                for n in range(count)
            ],
            axis=0,
        )
        index = index + tap_steps(index.shape)
        found = jnp.zeros(index.shape, f32)
        for start in range(0, FRAME_PIXELS, LANES):
            base = min(start, FRAME_PIXELS - LANES)
            part = frame[pl.ds(base, LANES), :]
            volume = lax.dot_general(q, part, (((1,), (1,)), ((), ())), preferred_element_type=f32)
            local = index - base
            inside = (index >= start) & (index < start + LANES)
            picked = jnp.take_along_axis(volume, local & (LANES - 1), axis=1)
            found = jnp.where(inside, picked, found)
        found = found * scale
        return [jnp.transpose(found[n * PIXELS : (n + 1) * PIXELS])[:16] for n in range(count)]

    for j in range(KEYFRAMES):
        q = jnp.concatenate([p[0] for p in pairs[j]], axis=0)
        pixel_rows = [p[1] for p in pairs[j]]
        for result, (_, _, out, n) in zip(look_up(q, pixel_rows, features.at[j]), pairs[j]):
            out[n, :, :PIXELS] = result
            out[n, :, PIXELS:] = jnp.zeros((16, LANES - PIXELS), f32)

    for k in range(LOOP_MOST):
        facts = chosen[k, PIXELS:].astype(f32)
        frame = jnp.max(facts[4:5]).astype(jnp.int32)
        (result,) = look_up(chosen[k, :PIXELS], [split_grid(facts[0:2])], features.at[frame])
        result = jnp.concatenate([result, jnp.zeros((16, LANES - PIXELS), f32)], axis=1)
        for row, fact in ((9, 5), (10, 6), (11, 7)):
            result = jnp.where(rows == row, jnp.broadcast_to(facts[fact : fact + 1], (16, LANES)), result)
        loops[k] = result


def sigmoid(x):
    return 0.5 * jnp.tanh(0.5 * x) + 0.5


def update(tm_count, sub_count, near, near_prev, near_next, loop_corr, hidden, context, grid, depth, moves, ends,
           gate_weight, gate_bias, cand_weight, cand_bias, corr_weight, flow_weight, motion_bias, head_weight, head_bias,
           correlation, new_hidden, revision, pose, gradient, depth_pose, depth_diagonal,
           taps, inputs, heads, sources, shifts, enc_weight):
    frame_total = tm_count * sub_count * KEYFRAMES
    first = (lax.axis_index("tm") * sub_count + lax.axis_index("sub")) * KEYFRAMES
    enc_weight[0:TAPS] = corr_weight[...]
    enc_weight[TAPS : TAPS + 2] = flow_weight[...]
    enc_weight[TAPS + 2 : TAPS + 3] = motion_bias[...]
    enc_weight[TAPS + 3 :] = jnp.zeros((16 - TAPS - 3, LANES), f32)
    head_rows = jnp.concatenate([head_weight[...].astype(f32), jnp.zeros((12, LANES), f32)], axis=0).astype(bf16)
    loop_source = lax.rem(ends[0, 0], KEYFRAMES)
    targets, valids = [], []
    for e in range(EDGES):
        if e < NEAR:
            source = first + e // 4
            target = first + e // 4 + neighbour_steps[e % 4]
        else:
            source, target = ends[0, 0], ends[0, 1]
        ok = jnp.where((target >= 0) & (target < frame_total), 1.0, 0.0).astype(f32)
        safe = jnp.clip(target, 0, frame_total - 1)
        for a in range(3):
            shifts[a, e : e + 1, :] = jnp.full((1, LANES), moves[a, safe] - moves[a, source], f32)
        shifts[3, e : e + 1, :] = jnp.full((1, LANES), ok, f32)
        valids.append(ok)
    shift_x, shift_y, shift_z, valid = [shifts[a, :EDGES, :PIXELS] for a in range(4)]

    lane = lax.broadcasted_iota(jnp.int32, (EDGES, PIXELS), 1)
    pixel_row = jnp.where(lane >= WIDTH, 1, 0)
    pixel_col = (lane - WIDTH * pixel_row).astype(f32)
    pixel_row = pixel_row.astype(f32)
    _, grid_row, grid_col = [value[:, :PIXELS] for value in split_rows(grid)]
    flow_u = (grid_col - pixel_col) / 40.0
    flow_v = (grid_row - pixel_row) / 40.0

    crossing = {e: near_next[n] for n, (e, _, _) in enumerate(TO_NEXT)}
    crossing.update({e: near_prev[n] for n, (e, _, _) in enumerate(TO_PREV)})
    low = lax.broadcasted_iota(jnp.int32, (16, PIXELS), 0)
    for e in range(EDGES):
        found = loop_corr[...] if e == NEAR else crossing[e] if e in crossing else near[e]
        found = found[:, :PIXELS] * valids[e]
        correlation[e, :, 0, :] = found[:TAPS, :WIDTH]
        correlation[e, :, 1, :] = found[:TAPS, WIDTH:]
        rows = jnp.where(low < TAPS, found, 0.0)
        rows = jnp.where(low == 9, jnp.broadcast_to(flow_u[e : e + 1], rows.shape), rows)
        rows = jnp.where(low == 10, jnp.broadcast_to(flow_v[e : e + 1], rows.shape), rows)
        rows = jnp.where(low == 11, 1.0, rows)
        motion = lax.dot_general(
            rows, enc_weight[...], (((0,), (0,)), ((), ())), precision=highest, preferred_element_type=f32
        )
        about = context[e // 4 if e < NEAR else loop_source].astype(f32)
        inputs[e] = (jax.nn.relu(motion) + about).astype(bf16).astype(f32)
        sources[e : e + 1] = flatten(depth[pl.ds(e // 4 if e < NEAR else loop_source, 1)])

    def halves(x):
        return x[:, :WIDTH].reshape(-1, LANES), x[:, WIDTH:].reshape(-1, LANES)

    count = EDGES * WIDTH
    col = lax.broadcasted_iota(jnp.int32, (EDGES, WIDTH, LANES), 1).reshape(count, LANES)

    def around(x):
        left = jnp.where(col == 0, 0.0, pltpu.roll(x, 1, 0))
        right = jnp.where(col == WIDTH - 1, 0.0, pltpu.roll(x, count - 1, 0))
        return left.astype(bf16), x.astype(bf16), right.astype(bf16)

    hid = halves(hidden[...].astype(f32))
    inp = halves(inputs[...])
    for r in range(2):
        for b, value in enumerate(around(hid[r])):
            taps[r, :, 2 * b * LANES : (2 * b + 1) * LANES] = value
        for b, value in enumerate(around(inp[r])):
            taps[r, :, (2 * b + 1) * LANES : (2 * b + 2) * LANES] = value
    dot = functools.partial(jnp.dot, preferred_element_type=f32)
    keep = []
    gated = []
    for r in range(2):
        gates = dot(taps[0], gate_weight[1 - r]) + dot(taps[1], gate_weight[2 - r]) + gate_bias[...]
        gates = sigmoid(gates)
        keep.append(gates[:, :LANES])
        gated.append((gates[:, LANES:] * hid[r]).astype(bf16).astype(f32))
    for r in range(2):
        for b, value in enumerate(around(gated[r])):
            taps[r, :, 2 * b * LANES : (2 * b + 1) * LANES] = value
    both = dot(taps[0], jnp.concatenate([cand_weight[1], cand_weight[0]], axis=1))
    both = both + dot(taps[1], jnp.concatenate([cand_weight[2], cand_weight[1]], axis=1))
    fresh = []
    for r in range(2):
        candidate = jnp.tanh(both[:, r * LANES : (r + 1) * LANES] + cand_bias[...])
        fresh.append(((1.0 - keep[r]) * hid[r] + keep[r] * candidate).reshape(EDGES, WIDTH, LANES))
    new_hidden[...] = jnp.concatenate(fresh, axis=1).astype(bf16)
    for e in range(EDGES):
        head = lax.dot_general(
            head_rows, new_hidden[e], (((1,), (1,)), ((), ())), preferred_element_type=f32
        )
        for h in range(4):
            heads[h, e : e + 1, :PIXELS] = head[h : h + 1]
    delta_u = heads[0, :EDGES, :PIXELS] + head_bias[0]
    delta_v = heads[1, :EDGES, :PIXELS] + head_bias[1]
    weight_u = sigmoid(heads[2, :EDGES, :PIXELS] + head_bias[2])
    weight_v = sigmoid(heads[3, :EDGES, :PIXELS] + head_bias[3])
    def halve(out, n, value):
        out[:, n, 0, :] = value[:, :WIDTH]
        out[:, n, 1, :] = value[:, WIDTH:]

    for h, value in enumerate((delta_u, delta_v, weight_u, weight_v)):
        halve(revision, h, value)

    d = sources[:EDGES, :PIXELS]
    x = (pixel_col - (WIDTH - 1) / 2.0) / 40.0
    y = (pixel_row - (HEIGHT - 1) / 2.0) / 40.0
    depth_u = shift_x - x * shift_z
    depth_v = shift_y - y * shift_z
    resid_u = (grid_col - (WIDTH - 1) / 2.0) / 40.0 + delta_u - (x + d * depth_u)
    resid_v = (grid_row - (HEIGHT - 1) / 2.0) / 40.0 + delta_v - (y + d * depth_v)
    jac_u = (d, None, -x * d, -x * y, 1.0 + x * x, -y)
    jac_v = (None, d, -y * d, -(1.0 + y * y), x * y, x)
    wu, wv = weight_u * valid, weight_v * valid
    six = lax.broadcasted_iota(jnp.int32, (EDGES, 6), 1)
    blocks = [jnp.zeros((EDGES, 6), f32)] * 6
    slopes = jnp.zeros((EDGES, 6), f32)
    zero = jnp.zeros_like(d)

    def both_terms(a, u, v):
        left = zero if jac_u[a] is None or u is None else jac_u[a] * u
        right = zero if jac_v[a] is None or v is None else jac_v[a] * v
        return left + right

    def put(total, value, k):
        return jnp.where(six == k, value, total)

    for a in range(6):
        u = None if jac_u[a] is None else jac_u[a] * wu
        v = None if jac_v[a] is None else jac_v[a] * wv
        for b in range(a, 6):
            value = jnp.sum(both_terms(b, u, v), axis=1, keepdims=True)
            blocks[a] = put(blocks[a], value, b)
            if b > a:
                blocks[b] = put(blocks[b], value, a)
        value = jnp.sum(both_terms(a, wu * resid_u, wv * resid_v), axis=1, keepdims=True)
        slopes = put(slopes, value, a)
        halve(depth_pose, a, both_terms(a, wu * depth_u, wv * depth_v))
    for a in range(6):
        pose[a] = jnp.transpose(blocks[a])
    gradient[...] = jnp.transpose(slopes)
    curvature = wu * depth_u * depth_u + wv * depth_v * depth_v
    slope = wu * depth_u * resid_u + wv * depth_v * resid_v
    for n, value in enumerate((curvature, slope)):
        for i in range(KEYFRAMES):
            extra = jnp.where(loop_source == i, value[NEAR:], 0.0)
            extra = extra + jnp.sum(value[4 * i : 4 * i + 4], axis=0, keepdims=True)
            depth_diagonal[i, n, 0:1, :] = extra[:, :WIDTH]
            depth_diagonal[i, n, 1:2, :] = extra[:, WIDTH:]


def on_device(tm_count, sub_count, feature_maps, context_maps, hidden_state, lookup_grid, loop_edges,
              inverse_depth, translations, update_reset_weight, update_reset_bias, candidate_weight,
              candidate_bias, correlation_weight, flow_weight, motion_bias, head_weight, head_bias):
    channels = feature_maps.shape[-1]
    shape = jax.ShapeDtypeStruct
    whole = pl.BlockSpec(memory_space=VMEM)
    scalar = pl.BlockSpec(memory_space=pltpu.SMEM)
    dma = pltpu.SemaphoreType.DMA
    near_msg = (QUERY_MSG, LANES)
    loop_msg = (LOOP_MSG, LANES)
    half = tm_count // 2
    heads_spec = pl.BlockSpec(
        (KEYFRAMES, QUERY_ROWS, WIDTH, channels), lambda i: (0, 0, 0, 0), memory_space=VMEM
    )
    from_prev, from_next, chosen = pl.pallas_call(
        functools.partial(queries_out, tm_count, sub_count),
        grid=(1,),
        out_shape=(shape(near_msg, bf16), shape(near_msg, bf16), shape((LOOP_MOST,) + loop_msg, bf16)),
        in_specs=[heads_spec, whole, scalar],
        out_specs=(whole,) * 3,
        scratch_shapes=[VMEM(near_msg, bf16)] * 4 + [
            VMEM((2, half, sub_count) + loop_msg, bf16),
            dma((2, 2)), dma((2, sub_count)), dma((2, half)), dma((2, half)),
        ],
        compiler_params=params(0),
        name="queries_out",
    )(feature_maps, lookup_grid, loop_edges)

    tap_shape = (16, LANES)
    near, res_prev, res_next, loops = pl.pallas_call(
        correlate,
        grid=(1,),
        out_shape=tuple(shape((n,) + tap_shape, f32) for n in (NEAR, 3, 3, LOOP_MOST)),
        in_specs=[whole, heads_spec] + [whole] * 4,
        out_specs=(whole,) * 4,
        compiler_params=params(),
        name="correlate",
    )(feature_maps.reshape(KEYFRAMES, FRAME_PIXELS, channels), feature_maps, lookup_grid, from_prev, from_next, chosen)

    near_prev, near_next, loop_corr = pl.pallas_call(
        functools.partial(results_back, tm_count, sub_count),
        out_shape=(shape((3,) + tap_shape, f32), shape((3,) + tap_shape, f32), shape(tap_shape, f32)),
        in_specs=[whole] * 3,
        out_specs=(whole,) * 3,
        scratch_shapes=[
            VMEM((3,) + tap_shape, f32), VMEM((3,) + tap_shape, f32),
            VMEM((sub_count, LOOP_MOST) + tap_shape, f32),
            VMEM((tm_count,) + tap_shape, f32), VMEM((tm_count,) + tap_shape, f32),
            dma((2, 2)), dma((2, tm_count)), dma((2, sub_count)),
        ],
        compiler_params=params(1),
        name="results_back",
    )(res_next, res_prev, loops)

    correlation, new_hidden, revision, pose, gradient, depth_pose, depth_diagonal = pl.pallas_call(
        functools.partial(update, tm_count, sub_count),
        out_shape=(
            shape((EDGES, TAPS, QUERY_ROWS, WIDTH), f32), shape((EDGES, PIXELS, LANES), bf16),
            shape((EDGES, 4, QUERY_ROWS, WIDTH), f32), shape((6, 6, EDGES), f32), shape((6, EDGES), f32),
            shape((EDGES, 6, QUERY_ROWS, WIDTH), f32), shape((KEYFRAMES, 2, QUERY_ROWS, WIDTH), f32),
        ),
        in_specs=[whole] * 8 + [scalar] * 2 + [whole] * 8 + [scalar],
        out_specs=(whole,) * 7,
        scratch_shapes=[
            VMEM((2, EDGES * WIDTH, 6 * LANES), bf16), VMEM((EDGES, PIXELS, LANES), f32),
            VMEM((4, 24, LANES), f32), VMEM((24, LANES), f32), VMEM((4, 24, LANES), f32), VMEM((16, LANES), f32),
        ],
        compiler_params=params(),
        name="update",
    )(
        near, near_prev, near_next, loop_corr, hidden_state.reshape(EDGES, PIXELS, LANES),
        context_maps.reshape(KEYFRAMES, PIXELS, LANES), lookup_grid, inverse_depth, translations, loop_edges,
        update_reset_weight.reshape(3, 6 * LANES, 2 * LANES), update_reset_bias[None],
        candidate_weight.reshape(3, 6 * LANES, LANES), candidate_bias[None], correlation_weight, flow_weight,
        motion_bias[None], head_weight.T, head_bias,
    )
    return (
        correlation, new_hidden.reshape(hidden_state.shape), revision, pose.transpose(2, 0, 1), gradient.T,
        depth_pose, depth_diagonal,
    )


def solution(mesh):
    lead = ("tm", "sub")
    over = lambda rank: P(lead, *([None] * (rank - 1)))
    in_specs = tuple(over(rank) for rank in (4, 4, 4, 3, 2, 3)) + (P(),) * 10
    out_specs = tuple(over(rank) for rank in (4, 4, 4, 3, 2, 4, 4))
    return jax.shard_map(
        functools.partial(on_device, mesh.shape["tm"], mesh.shape["sub"]),
        mesh=mesh, in_specs=in_specs, out_specs=out_specs, check_vma=False,
    )
```
